32 devices in a mesh: seq: 4 (over y, core), head: 8 (over z, x).
Axes of the slice: x: 2, y: 2, z: 4, core: 2. Of those that a mesh axis runs over, the one named last changes fastest.
Arguments:
- query_latent: bfloat16 [1024, 128, 576], P('seq', 'head'), may hold values from -6 to 6
- key_latent: bfloat16 [512, 576], P('seq'), may hold values from -6 to 6
- normalizer: float32 [1024, 128], P('seq', 'head'), may hold values from 7 to 9
- index_query: bfloat16 [1024, 64, 128], P('seq', 'head'), may hold values from -20 to 20
- index_key: bfloat16 [512, 128], P('seq'), may hold values from -6.5 to 6.5
- index_weight: float32 [1024, 64], P('seq', 'head'), may hold values from 0.05 to 0.5
- kept: int32 [8, 4], P('seq'), may hold values from 0 to 1, as said below
Outputs:
- index_query_grad: bfloat16 [1024, 64, 128], P('seq', 'head')
- index_key_grad: float32 [512, 128], P('seq')
The draws below stay inside these ranges and needn't reach their ends.
Inputs may be any that keep to these rules, and one draw needn't show every extreme that they name: `kept`: every query tile keeps the key tile whose position matches its own block of 256 queries.
All inputs are finite; a program needn't handle non-finite values.
Results may differ from the reference program's by a relative error of at most 0.009.
Values may be sent and summed in bfloat16 or wider, within the bound.
A program may use at most 64 MiB of HBM per device.

```python
import math
import jax
import jax.numpy as jnp
from jax import lax

H = 128
LATENT = 512
ROPE = 64
IH = 64
ID = 128
TILE = 128
Q_DEV = 256
QUERIES = 1024
KEYS = 512
N_SEQ = 4


def base_keys(key):
    values = jax.random.normal(jax.random.fold_in(key, 7), (KEYS, ID), jnp.float32)
    return jnp.clip(values, -6.0, 6.0)


def draw_index_key(key, part):
    values = base_keys(key)
    return values.astype(jnp.bfloat16)


def draw_index_query(key, part):
    values = jax.random.normal(jax.random.fold_in(key, 11), (QUERIES, IH, ID), jnp.float32)
    values = jnp.clip(values, -6.0, 6.0)
    return values.astype(jnp.bfloat16)


def draw_kept(key, part):
    tiles = QUERIES // TILE
    rate = jax.random.randint(jax.random.fold_in(key, 3), (tiles, 1), 55, 101)
    roll = jax.random.randint(jax.random.fold_in(key, 5), (tiles, N_SEQ), 0, 100)
    own_tile = jnp.arange(tiles)[:, None] // (Q_DEV // TILE) == jnp.arange(N_SEQ)[None, :]
    return jnp.where(own_tile | (roll < rate), 1, 0).astype(jnp.int32)


def block_levels(own_key, shape, shards, smallest, largest):
    level = 1.0
    for axis_at, blocks in shards:
        steps = jax.random.uniform(jax.random.fold_in(jax.random.fold_in(own_key, 6), axis_at), (blocks,), jnp.float32, smallest / len(shards), largest / len(shards))
        level = level * jnp.repeat(jnp.exp(steps), shape[axis_at] // blocks).reshape((-1,) + (1,) * (len(shape) - 1 - axis_at))
    return level


def centred(rng, shape, scale, bound, pieces=(), dtype=jnp.bfloat16):
    level = block_levels(rng, shape, pieces, -0.22, 0.18) if pieces else 1.0
    values = jax.random.normal(rng, shape, jnp.float32) * scale * level
    return jnp.minimum(jnp.maximum(values, -bound), bound).astype(dtype)


def setup_inputs(seed: int = 0) -> dict:
    key_list = jax.random.split(jax.random.key(seed), 8)
    return {
        "query_latent": centred(key_list[0], (QUERIES, H, LATENT + ROPE), 1.0, 6.0, ((0, 4), (1, 8))),
        "key_latent": centred(key_list[1], (KEYS, LATENT + ROPE), 1.0, 6.0, ((0, 4),)),
        "normalizer": jnp.clip(7.0 + 2.0 * jax.random.uniform(key_list[2], (QUERIES, H), jnp.float32) ** block_levels(key_list[2], (QUERIES, H), ((0, 4), (1, 8)), -0.2, 0.2), 7.0, 9.0),
        "index_query": draw_index_query(jax.random.fold_in(key_list[7], 71), 0),
        "index_key": draw_index_key(jax.random.fold_in(key_list[7], 71), 0),
        "index_weight": jnp.clip(jnp.exp(math.log(0.5) - 2.3025851 * jax.random.uniform(key_list[5], (QUERIES, IH), jnp.float32) ** block_levels(key_list[5], (QUERIES, IH), ((0, 4), (1, 8)), -0.2, 0.2)), 0.05, 0.5),
        "kept": draw_kept(jax.random.fold_in(key_list[7], 71), 0),
    }


attn_scale = 192.0 ** -0.5


def reference(query_latent, key_latent, normalizer, index_query, index_key, index_weight, kept):
    tiles = QUERIES // TILE
    width = LATENT + ROPE
    index_scale = ID ** -0.5
    allow_cols = jnp.repeat(kept, TILE, axis=1) > 0
    query_tiles = query_latent.reshape(tiles, TILE, H, width)
    norm_tiles = normalizer.reshape(tiles, TILE, H)
    iquery_tiles = index_query.reshape(tiles, TILE, IH, ID)
    weight_tiles = index_weight.reshape(tiles, TILE, IH)
    keys_f = index_key.astype(jnp.float32)

    def one_tile(carry, parts):
        query, lse, iquery, weight, keep = parts
        scores = jnp.dot(query.reshape(TILE * H, width), key_latent.T, preferred_element_type=jnp.float32) * attn_scale
        prob = jnp.exp(scores.reshape(TILE, H, KEYS) - lse[:, :, None])
        head_sum = jnp.where(keep[None, :], jnp.sum(prob, axis=1), 0.0)
        target = head_sum / jnp.sum(head_sum, axis=1, keepdims=True)
        z_val = jnp.einsum('tjd,sd->tjs', iquery.astype(jnp.float32), keys_f) * index_scale
        logit = jnp.sum(weight[:, :, None] * jnp.maximum(z_val, 0.0), axis=1)
        top = jnp.max(jnp.where(keep[None, :], logit, -jnp.inf), axis=1, keepdims=True)
        expo = jnp.where(keep[None, :], jnp.exp(jnp.where(keep[None, :], logit, top) - top), 0.0)
        iprob = expo / jnp.sum(expo, axis=1, keepdims=True)
        gradient = iprob - target
        dz_val = jnp.where(z_val > 0, gradient[:, None, :] * weight[:, :, None], 0.0).astype(jnp.bfloat16)
        dz_f = dz_val.astype(jnp.float32)
        dquery = (jnp.einsum('tjs,sd->tjd', dz_f, keys_f) * index_scale).astype(jnp.bfloat16)
        dkey = jnp.einsum('tjs,tjd->sd', dz_f, iquery.astype(jnp.float32)) * index_scale
        return carry + dkey, dquery

    start = jnp.zeros((KEYS, ID), jnp.float32)
    dkey, dquery = lax.scan(one_tile, start, (query_tiles, norm_tiles, iquery_tiles, weight_tiles, allow_cols))
    return dquery.reshape(QUERIES, IH, ID), dkey
```

```python
import functools
import jax
import jax.numpy as jnp
from jax import lax
from jax.experimental import pallas as pl
from jax.experimental.pallas import tpu as pltpu
from jax.sharding import PartitionSpec as P

attn_scale = 192.0 ** (-0.5)
MESH = pl.DeviceIdType.MESH
F32 = jnp.float32
BF16 = jnp.bfloat16


def dot(a, b, ca, cb):
    return lax.dot_general(a, b, (((ca,), (cb,)), ((), ())), preferred_element_type=F32)


def column(ref_rows, heads):
    rows = ref_rows.shape[0]
    wide = jnp.broadcast_to(ref_rows[:, None, :], (rows, heads, heads))
    sub = lax.broadcasted_iota(jnp.int32, (rows, heads, heads), 1)
    lane = lax.broadcasted_iota(jnp.int32, (rows, heads, heads), 2)
    return jnp.sum(jnp.where(sub == lane, wide, 0.0), axis=2, keepdims=True)


def kernel(
    ns, nh, heads, iheads, index_scale,
    q_hbm, kl_ref, nrm_ref, iq_ref, ik_ref, w_ref, kept_ref,
    dq_ref, dk_ref,
    qbuf, klat, keys, wm,
    s1l, s1h, r1l, r1h, s2l, s2h, r2l, r2h, gall, acc,
    sa, ra, sb, rb, rc,
    q_sem, ik_send, ik_recv, kl_send, kl_recv,
    l1_send, l1_recv, h1_send, h1_recv, l2_send, l2_recv, h2_send, h2_recv,
    g_send, g_fsend, g_recv, a_send, a_recv, b_send, b_recv, c_send, c_recv,
):
    me_s, me_h = lax.axis_index("seq"), lax.axis_index("head")
    half = nh // 2
    mz, mx = me_h // 2, me_h % 2
    px = 1 - mx
    pair = mz * 2 + px
    n_keys, kb = klat.shape[0], kl_ref.shape[0]
    cr = r1l.shape[1]
    qr, wr = cr * heads, cr * iheads

    def chunk_of(i):
        first = i < half
        zt = (mz + 1 + i) % half
        return zt, jnp.where(first, px, mx) * half + zt

    def copy(src, dst, ss, rs, s, h):
        return pltpu.make_async_remote_copy(
            src_ref=src, dst_ref=dst, send_sem=ss, recv_sem=rs,
            device_id=(s, h), device_id_type=MESH,
        )

    def q_copy(i):
        _, k = chunk_of(i)
        return pltpu.make_async_copy(q_hbm.at[pl.ds(k * qr, qr)], qbuf.at[i], q_sem.at[i])

    for i in range(nh):
        q_copy(i).start()

    barrier = pltpu.get_barrier_semaphore()
    for d in range(1, ns):
        pl.semaphore_signal(barrier, inc=1, device_id=((me_s + d) % ns, me_h), device_id_type=MESH)
    for d in range(1, nh):
        pl.semaphore_signal(barrier, inc=1, device_id=(me_s, (me_h + d) % nh), device_id_type=MESH)
    pl.semaphore_wait(barrier, ns - 1 + nh - 1)

    def own_rows(s):
        return pl.ds(pl.multiple_of(s * kb, kb), kb)

    def ik_copy(d, s):
        return copy(ik_ref, keys.at[own_rows(s)], ik_send.at[d], ik_recv.at[s], (me_s + d) % ns, me_h)

    def kl_copy(d, s):
        return copy(kl_ref, klat.at[own_rows(s)], kl_send.at[d], kl_recv.at[s], (me_s + d) % ns, me_h)

    for d in range(1, ns):
        ik_copy(d, me_s).start()
    for d in range(1, ns):
        kl_copy(d, me_s).start()
    keys[own_rows(me_s), :] = ik_ref[...]
    klat[own_rows(me_s), :] = kl_ref[...]
    for d in range(1, ns):
        ik_copy(d, (me_s + d) % ns).wait_recv()
    for d in range(1, ns):
        kl_copy(d, (me_s + d) % ns).wait_recv()

    def l1_copy(zt):
        return copy(s1l.at[zt], r1l.at[zt], l1_send.at[zt], l1_recv.at[zt], me_s, pair)

    def h1_copy(zt):
        return copy(s1h.at[zt], r1h.at[zt], h1_send.at[zt], h1_recv.at[zt], me_s, pair)

    def l2_copy(zt, frm):
        return copy(s2l.at[zt], r2l.at[frm], l2_send.at[zt], l2_recv.at[frm], me_s, zt * 2 + mx)

    def h2_copy(zt, frm):
        return copy(s2h.at[zt], r2h.at[frm], h2_send.at[zt], h2_recv.at[frm], me_s, zt * 2 + mx)

    def step(i, _):
        zt, k = chunk_of(i)
        rows = pl.ds(pl.multiple_of(k * cr, cr), cr)
        wide = pl.ds(pl.multiple_of(k * wr, wr), wr)
        z = dot(iq_ref[wide, :], keys[...], 1, 1).reshape(cr, iheads, n_keys)
        part = jnp.where(z > 0, column(w_ref[rows, :], iheads), 0.0)
        wm[k] = part.reshape(wr, n_keys)
        logit = jnp.sum(part * z, axis=1) * index_scale

        @pl.when(i < half)
        def _():
            s1l[zt] = logit
            l1_copy(zt).start()

        q_copy(i).wait()
        scores = dot(qbuf[i], klat[...], 1, 1).reshape(cr, heads, n_keys)
        prob = jnp.exp(scores * attn_scale - column(nrm_ref[rows, :], heads))
        value = jnp.sum(prob, axis=1)

        @pl.when(i < half)
        def _():
            s1h[zt] = value.astype(BF16)
            h1_copy(zt).start()

        @pl.when(i >= half)
        def _():
            l1_copy(zt).wait_recv()
            s2l[zt] = logit + r1l[zt]

            @pl.when(i < nh - 1)
            def _():
                l2_copy(zt, mz).start()

            h1_copy(zt).wait_recv()
            s2h[zt] = (value + r1h[zt].astype(F32)).astype(BF16)

            @pl.when(i < nh - 1)
            def _():
                h2_copy(zt, mz).start()

        return 0

    lax.fori_loop(0, nh, step, 0)

    logit = s2l[mz]
    head_sum = s2h[mz].astype(F32)
    for d in range(1, half):
        frm = (mz + half - d) % half
        l2_copy(frm, frm).wait_recv()
        logit = logit + r2l[frm]
    for d in range(1, half):
        frm = (mz + half - d) % half
        h2_copy(frm, frm).wait_recv()
        head_sum = head_sum + r2h[frm].astype(F32)

    mine = mx * half + mz
    tile_rows = (cr * nh) // kept_ref.shape[0]
    tile_at = (mine * cr) // tile_rows
    kt = n_keys // kept_ref.shape[1]
    keep = jnp.concatenate(
        [jnp.full((cr, kt), kept_ref[tile_at, j], jnp.int32) for j in range(kept_ref.shape[1])],
        axis=1,
    ) > 0
    head_sum = jnp.where(keep, head_sum, 0.0)
    target = head_sum / jnp.sum(head_sum, axis=1, keepdims=True)
    top = jnp.max(jnp.where(keep, logit, -jnp.inf), axis=1, keepdims=True)
    expo = jnp.where(keep, jnp.exp(jnp.where(keep, logit, top) - top), 0.0)
    gall[mine] = (expo / jnp.sum(expo, axis=1, keepdims=True) - target).astype(BF16)

    def g_copy(d, k):
        zt = (mz + d) % half
        return copy(gall.at[k], gall.at[k], g_send.at[d], g_recv.at[k], me_s, zt * 2 + mx)

    def g_pass(d, k):
        return copy(gall.at[k], gall.at[k], g_fsend.at[d], g_recv.at[k], me_s, pair)

    for d in range(1, half):
        g_copy(d, mine).start()
    g_pass(0, mine).start()

    acc[...] = jnp.zeros_like(acc)

    def backward(k):
        wide = pl.ds(pl.multiple_of(k * wr, wr), wr)
        g = gall[k].astype(F32)
        dz = (g[:, None, :] * wm[k].reshape(cr, iheads, n_keys)).astype(BF16).reshape(wr, n_keys)
        dq_ref[wide, :] = (dot(dz, keys[...], 1, 0) * index_scale).astype(BF16)
        acc[...] += dot(iq_ref[wide, :], dz, 0, 0)

    def back_step(i, _):
        zt = (mz + half - i % half) % half
        k = jnp.where(i < half, mx, px) * half + zt

        @pl.when(jnp.logical_and(i > 0, i < half))
        def _():
            g_copy(i, k).wait_recv()
            g_pass(i, k).start()

        @pl.when(i >= half)
        def _():
            g_pass(i - half, k).wait_recv()

        backward(k)
        return 0

    lax.fori_loop(0, nh, back_step, 0)

    wire = sb.dtype
    br = rb.shape[1]

    def a_copy(d, s):
        return copy(sa.at[d], ra.at[s], a_send.at[d], a_recv.at[s], (me_s + d) % ns, me_h)

    for d in range(1, ns):
        sa[d] = (acc[:, own_rows((me_s + d) % ns)] * index_scale).astype(BF16)
        a_copy(d, me_s).start()
    total = acc[:, own_rows(me_s)] * index_scale
    for d in range(1, ns):
        a_copy(d, (me_s + d) % ns).wait_recv()
        total = total + ra[(me_s + d) % ns].astype(F32)
    sb[...] = total.astype(wire)

    def b_rows(h):
        return pl.ds(pl.multiple_of(h * br, br), br)

    def b_copy(d, h):
        to = (me_h + d) % nh
        return copy(sb.at[b_rows(to)], rb.at[h], b_send.at[d], b_recv.at[h], me_s, to)

    def c_copy(d, h):
        return copy(rc.at[b_rows(h)], rc.at[b_rows(h)], c_send.at[d], c_recv.at[h], me_s, (me_h + d) % nh)

    for d in range(1, nh):
        b_copy(d, me_h).start()
    piece = sb[b_rows(me_h), :].astype(F32)
    for d in range(1, nh):
        frm = (me_h + d) % nh
        b_copy(d, frm).wait_recv()
        piece = piece + rb[frm].astype(F32)
    rc[b_rows(me_h), :] = piece.astype(wire)
    for d in range(1, nh):
        c_copy(d, me_h).start()
    for d in range(1, nh):
        c_copy(d, (me_h + d) % nh).wait_recv()
    dk_ref[...] = rc[...].astype(F32).T

    for d in range(1, ns):
        ik_copy(d, me_s).wait_send()
        kl_copy(d, me_s).wait_send()
        a_copy(d, me_s).wait_send()
    for i in range(half):
        l1_copy(i).wait_send()
        h1_copy(i).wait_send()
        g_pass(i, mine).wait_send()
    for d in range(1, half):
        zt = (mz + d) % half
        l2_copy(zt, mz).wait_send()
        h2_copy(zt, mz).wait_send()
        g_copy(d, mine).wait_send()
    for d in range(1, nh):
        b_copy(d, me_h).wait_send()
        c_copy(d, me_h).wait_send()


def local(ns, nh, query_latent, key_latent, normalizer, index_query, index_key, index_weight, kept):
    t, heads, width = query_latent.shape
    ihead, idim = index_query.shape[1:]
    iheads = -(-ihead // 8) * 8
    if iheads != ihead:
        index_query = jnp.pad(index_query, ((0, 0), (0, iheads - ihead), (0, 0)))
        index_weight = jnp.pad(index_weight, ((0, 0), (0, iheads - ihead)))
    kb = key_latent.shape[0]
    n_keys = kb * ns
    cr, half, br = t // nh, nh // 2, idim // nh
    wire = BF16 if br % 16 == 0 else F32
    vmem, dma = pltpu.VMEM, pltpu.SemaphoreType.DMA
    in_vmem = pl.BlockSpec(memory_space=pltpu.VMEM)
    dq, dk = pl.pallas_call(
        functools.partial(kernel, ns, nh, heads, iheads, idim ** (-0.5)),
        out_shape=(
            jax.ShapeDtypeStruct((t * iheads, idim), BF16),
            jax.ShapeDtypeStruct((kb, idim), F32),
        ),
        in_specs=[pl.BlockSpec(memory_space=pl.ANY)] + [in_vmem] * 5
        + [pl.BlockSpec(memory_space=pltpu.SMEM)],
        out_specs=(in_vmem, in_vmem),
        scratch_shapes=[
            vmem((nh, cr * heads, width), BF16),
            vmem((n_keys, width), BF16),
            vmem((n_keys, idim), BF16),
            vmem((nh, cr * iheads, n_keys), F32),
            vmem((half, cr, n_keys), F32),
            vmem((half, cr, n_keys), BF16),
            vmem((half, cr, n_keys), F32),
            vmem((half, cr, n_keys), BF16),
            vmem((half, cr, n_keys), F32),
            vmem((half, cr, n_keys), BF16),
            vmem((half, cr, n_keys), F32),
            vmem((half, cr, n_keys), BF16),
            vmem((nh, cr, n_keys), BF16),
            vmem((idim, n_keys), F32),
            vmem((ns, idim, kb), BF16),
            vmem((ns, idim, kb), BF16),
            vmem((idim, kb), wire),
            vmem((nh, br, kb), wire),
            vmem((idim, kb), wire),
            dma((nh,)), dma((ns,)), dma((ns,)), dma((ns,)), dma((ns,)),
            dma((half,)), dma((half,)), dma((half,)), dma((half,)),
            dma((half,)), dma((half,)), dma((half,)), dma((half,)),
            dma((half,)), dma((half,)), dma((nh,)),
            dma((ns,)), dma((ns,)), dma((nh,)), dma((nh,)), dma((nh,)), dma((nh,)),
        ],
        compiler_params=pltpu.CompilerParams(
            collective_id=0, has_side_effects=True, vmem_limit_bytes=56 * 1024 * 1024
        ),
    )(
        query_latent.reshape(t * heads, width), key_latent, normalizer,
        index_query.reshape(t * iheads, idim), index_key, index_weight, kept,
    )
    dq = dq.reshape(t, iheads, idim)
    return (dq[:, :ihead] if iheads != ihead else dq), dk


def solution(mesh):
    ns, nh = mesh.shape["seq"], mesh.shape["head"]
    return jax.shard_map(
        functools.partial(local, ns, nh),
        mesh=mesh,
        in_specs=(
            P("seq", "head", None),
            P("seq", None),
            P("seq", "head"),
            P("seq", "head", None),
            P("seq", None),
            P("seq", "head"),
            P("seq", None),
        ),
        out_specs=(P("seq", "head", None), P("seq", None)),
        check_vma=False,
    )
```

```python
import functools
import jax
import jax.numpy as jnp
from jax import lax
from jax.experimental import pallas as pl
from jax.experimental.pallas import tpu as pltpu
from jax.sharding import PartitionSpec as P

attn_scale = 192.0 ** (-0.5)
MESH = pl.DeviceIdType.MESH
F32 = jnp.float32
BF16 = jnp.bfloat16


def dot(a, b, ca, cb):
    return lax.dot_general(a, b, (((ca,), (cb,)), ((), ())), preferred_element_type=F32)


def kernel(
    ns, nh, heads, iheads, index_scale, group,
    q_hbm, kl_ref, nrm_ref, iq_hbm, ik_ref, w_ref, kept_ref,
    dq_hbm, dk_ref,
    qbuf, iq_ref, klat, keys, wm, w_col, hacc,
    s1l, r1l, s2l, r2l, s1h, r1h, own_h, s2h, r2h, gall, dz_ref, dq_ref, acc,
    sa, ra, sb, rb, rc,
    q_sem, iq_sem, dq_sem, ik_send, ik_recv, kl_send, kl_recv,
    l1_send, l1_recv, h1_send, h1_recv, l2_send, l2_recv, h2_send, h2_recv,
    g_send, g_fsend, g_recv, a_send, a_recv, b_send, b_recv, c_send, c_recv,
):
    me_s, me_h = lax.axis_index("seq"), lax.axis_index("head")
    half = nh // 2
    mz, mx = me_h // 2, me_h % 2
    px = 1 - mx
    pair = mz * 2 + px
    n_keys, kb = klat.shape[0], ik_ref.shape[0]
    cr = r1l.shape[1]
    hr = cr * half
    wr = cr * iheads
    nb, bk = s1h.shape[0], s1h.shape[2]

    def copy(src, dst, ss, rs, s, h):
        return pltpu.make_async_remote_copy(
            src_ref=src, dst_ref=dst, send_sem=ss, recv_sem=rs,
            device_id=(s, h), device_id_type=MESH,
        )

    iq_copy = pltpu.make_async_copy(iq_hbm, iq_ref, iq_sem)
    iq_copy.start()
    q_parts = q_sem.shape[0]
    qh = heads // q_parts

    def q_copy(i):
        return pltpu.make_async_copy(
            q_hbm.at[pl.ds(i * qh, qh)], qbuf.at[pl.ds(i * qh, qh)], q_sem.at[i]
        )

    for i in range(q_parts):
        q_copy(i).start()

    barrier = pltpu.get_barrier_semaphore()
    for d in range(1, ns):
        pl.semaphore_signal(barrier, inc=1, device_id=((me_s + d) % ns, me_h), device_id_type=MESH)
    for d in range(1, nh):
        pl.semaphore_signal(barrier, inc=1, device_id=(me_s, (me_h + d) % nh), device_id_type=MESH)

    def own_rows(s):
        return pl.ds(pl.multiple_of(s * kb, kb), kb)

    klat[own_rows(me_s), :] = kl_ref[...].T
    keys[own_rows(me_s), :] = ik_ref[...]
    w_col[...] = w_ref[...].T
    pl.semaphore_wait(barrier, ns - 1 + nh - 1)

    def ik_copy(d, s):
        rows = own_rows(s)
        return copy(keys.at[rows], keys.at[rows], ik_send.at[d], ik_recv.at[s], (me_s + d) % ns, me_h)

    def kl_copy(d, s):
        rows = own_rows(s)
        return copy(klat.at[rows], klat.at[rows], kl_send.at[d], kl_recv.at[s], (me_s + d) % ns, me_h)

    for d in range(1, ns):
        ik_copy(d, me_s).start()
    for d in range(1, ns):
        kl_copy(d, me_s).start()
    iq_copy.wait()
    for d in range(1, ns):
        ik_copy(d, (me_s + d) % ns).wait_recv()

    def l1_copy(zt):
        return copy(s1l.at[zt], r1l.at[zt], l1_send.at[zt], l1_recv.at[zt], me_s, pair)

    def l2_copy(zt, frm):
        return copy(s2l.at[zt], r2l.at[frm], l2_send.at[zt], l2_recv.at[frm], me_s, zt * 2 + mx)

    def h1_copy(b):
        return copy(s1h.at[b], r1h.at[b], h1_send.at[b], h1_recv.at[b], me_s, pair)

    def h2_copy(b, zt, frm):
        rows = pl.ds(pl.multiple_of(zt * cr, cr), cr)
        return copy(
            s2h.at[b, rows], r2h.at[frm, b], h2_send.at[b, zt], h2_recv.at[b, frm], me_s, zt * 2 + mx
        )

    def z_step(i, _):
        zt = (mz + 1 + i) % half
        k = jnp.where(i < half, px, mx) * half + zt
        rows = pl.ds(pl.multiple_of(k * cr, cr), cr)
        wide = pl.ds(pl.multiple_of(k * wr, wr), wr)
        z = dot(iq_ref[wide, :], keys[...], 1, 1).reshape(cr, iheads, n_keys)
        wide_w = jnp.broadcast_to(w_col[rows, :][:, None, :], (cr, iheads, iheads))
        sub = lax.broadcasted_iota(jnp.int32, (cr, iheads, iheads), 1)
        lane = lax.broadcasted_iota(jnp.int32, (cr, iheads, iheads), 2)
        w = jnp.sum(jnp.where(sub == lane, wide_w, 0.0), axis=2, keepdims=True)
        part = jnp.where(z > 0, w, 0.0)
        wm[k] = part.reshape(wr, n_keys)
        logit = jnp.sum(part * z, axis=1) * index_scale

        @pl.when(i < half)
        def _():
            s1l[zt] = logit
            l1_copy(zt).start()

        @pl.when(i >= half)
        def _():
            s2l[zt] = logit

        return 0

    lax.fori_loop(0, nh, z_step, 0)

    for d in range(1, ns):
        kl_copy(d, (me_s + d) % ns).wait_recv()
    for i in range(q_parts):
        q_copy(i).wait()

    def half_rows(x):
        return pl.ds(pl.multiple_of(x * hr, hr), hr)

    def pass_logits():
        for d in range(1, half + 1):
            zt = (mz + d) % half
            l1_copy(zt).wait_recv()
            s2l[zt] = s2l[zt] + r1l[zt]
            if d < half:
                l2_copy(zt, mz).start()

    def pass_sums(b):
        h1_copy(b).wait_recv()
        s2h[b] = (own_h[b] + r1h[b].astype(F32)).astype(BF16)
        for d in range(1, half):
            h2_copy(b, (mz + d) % half, mz).start()

    for b in range(nb):
        hacc[...] = jnp.zeros_like(hacc)

        def score_step(i, _):
            total = hacc[...]
            for j in range(group):
                h = i * group + j
                s = dot(klat[b * bk:(b + 1) * bk, :], qbuf[h], 1, 0)
                total = total + jnp.exp(s * attn_scale - nrm_ref[pl.ds(h, 1), :])
            hacc[...] = total
            return 0

        lax.fori_loop(0, heads // group, score_step, 0)
        turned = hacc[...].T
        low, high = turned[:hr], turned[hr:]
        s1h[b] = jnp.where(px == 0, low, high).astype(BF16)
        h1_copy(b).start()
        own_h[b] = jnp.where(mx == 0, low, high)
        if b == 0:
            pass_logits()
        if b > 0:
            pass_sums(b - 1)
    pass_sums(nb - 1)

    logit = s2l[mz]
    for d in range(1, half):
        frm = (mz + half - d) % half
        l2_copy(frm, frm).wait_recv()
        logit = logit + r2l[frm]

    mine = mx * half + mz
    tile_rows = (cr * nh) // kept_ref.shape[0]
    tile_at = (mine * cr) // tile_rows
    kt = n_keys // kept_ref.shape[1]
    keep = jnp.concatenate(
        [jnp.full((cr, kt), kept_ref[tile_at, j], jnp.int32) for j in range(kept_ref.shape[1])],
        axis=1,
    ) > 0
    top = jnp.max(jnp.where(keep, logit, -jnp.inf), axis=1, keepdims=True)
    expo = jnp.where(keep, jnp.exp(jnp.where(keep, logit, top) - top), 0.0)
    iprob = expo / jnp.sum(expo, axis=1, keepdims=True)

    sums = []
    for b in range(nb):
        value = s2h[b, pl.ds(pl.multiple_of(mz * cr, cr), cr)].astype(F32)
        for d in range(1, half):
            frm = (mz + half - d) % half
            h2_copy(b, frm, frm).wait_recv()
            value = value + r2h[frm, b].astype(F32)
        sums.append(value)
    head_sum = jnp.where(keep, jnp.concatenate(sums, axis=1), 0.0)
    target = head_sum / jnp.sum(head_sum, axis=1, keepdims=True)
    gall[mine] = (iprob - target).astype(BF16)

    def g_copy(d, k):
        zt = (mz + d) % half
        return copy(gall.at[k], gall.at[k], g_send.at[d], g_recv.at[k], me_s, zt * 2 + mx)

    def g_pass(d, k):
        return copy(gall.at[k], gall.at[k], g_fsend.at[d], g_recv.at[k], me_s, pair)

    for d in range(1, half):
        g_copy(d, mine).start()
    g_pass(0, mine).start()

    acc[...] = jnp.zeros_like(acc)

    def back_step(i, _):
        zt = (mz + half - i % half) % half
        k = jnp.where(i < half, mx, px) * half + zt

        @pl.when(jnp.logical_and(i > 0, i < half))
        def _():
            g_copy(i, k).wait_recv()
            g_pass(i, k).start()

        @pl.when(i >= half)
        def _():
            g_pass(i - half, k).wait_recv()

        wide = pl.ds(pl.multiple_of(k * wr, wr), wr)
        g = gall[k].astype(F32)
        dz = (g[:, None, :] * wm[k].reshape(cr, iheads, n_keys)).astype(BF16).reshape(wr, n_keys)
        dz_ref[wide, :] = dz
        acc[...] += dot(iq_ref[wide, :], dz, 0, 0)
        return 0

    lax.fori_loop(0, nh, back_step, 0)

    wire = sb.dtype
    br = rb.shape[1]

    def a_copy(d, s):
        return copy(sa.at[d], ra.at[s], a_send.at[d], a_recv.at[s], (me_s + d) % ns, me_h)

    for d in range(1, ns):
        sa[d] = (acc[:, own_rows((me_s + d) % ns)] * index_scale).astype(BF16)
        a_copy(d, me_s).start()

    def dq_copy(i):
        wide = pl.ds(i * wr, wr)
        return pltpu.make_async_copy(dq_ref.at[wide], dq_hbm.at[wide], dq_sem.at[i])

    def dq_step(i, _):
        wide = pl.ds(pl.multiple_of(i * wr, wr), wr)
        dq_ref[wide, :] = (dot(dz_ref[wide, :], keys[...], 1, 0) * index_scale).astype(BF16)
        dq_copy(i).start()
        return 0

    lax.fori_loop(0, half, dq_step, 0)

    total = acc[:, own_rows(me_s)] * index_scale
    for d in range(1, ns):
        a_copy(d, (me_s + d) % ns).wait_recv()
        total = total + ra[(me_s + d) % ns].astype(F32)
    sb[...] = total.astype(wire)

    def b_rows(h):
        return pl.ds(pl.multiple_of(h * br, br), br)

    def b_copy(d, h):
        to = (me_h + d) % nh
        return copy(sb.at[b_rows(to)], rb.at[h], b_send.at[d], b_recv.at[h], me_s, to)

    def c_copy(d, h):
        return copy(rc.at[b_rows(h)], rc.at[b_rows(h)], c_send.at[d], c_recv.at[h], me_s, (me_h + d) % nh)

    for d in range(1, nh):
        b_copy(d, me_h).start()

    lax.fori_loop(half, nh, dq_step, 0)

    piece = sb[b_rows(me_h), :].astype(F32)
    for d in range(1, nh):
        frm = (me_h + d) % nh
        b_copy(d, frm).wait_recv()
        piece = piece + rb[frm].astype(F32)
    rc[b_rows(me_h), :] = piece.astype(wire)
    for d in range(1, nh):
        c_copy(d, me_h).start()
    for d in range(1, nh):
        c_copy(d, (me_h + d) % nh).wait_recv()
    dk_ref[...] = rc[...].astype(F32).T

    for i in range(nh):
        dq_copy(i).wait()
    for d in range(1, ns):
        ik_copy(d, me_s).wait_send()
        kl_copy(d, me_s).wait_send()
        a_copy(d, me_s).wait_send()
    for i in range(half):
        l1_copy(i).wait_send()
        g_pass(i, mine).wait_send()
    for b in range(nb):
        h1_copy(b).wait_send()
    for d in range(1, half):
        zt = (mz + d) % half
        l2_copy(zt, mz).wait_send()
        g_copy(d, mine).wait_send()
        for b in range(nb):
            h2_copy(b, zt, mz).wait_send()
    for d in range(1, nh):
        b_copy(d, me_h).wait_send()
        c_copy(d, me_h).wait_send()


def local(ns, nh, query_latent, key_latent, normalizer, index_query, index_key, index_weight, kept):
    t, heads, width = query_latent.shape
    ihead, idim = index_query.shape[1:]
    iheads = -(-ihead // 8) * 8
    if iheads != ihead:
        index_query = jnp.pad(index_query, ((0, 0), (0, iheads - ihead), (0, 0)))
        index_weight = jnp.pad(index_weight, ((0, 0), (0, iheads - ihead)))
    kb = key_latent.shape[0]
    n_keys = kb * ns
    cr, half, br = t // nh, nh // 2, idim // nh
    wire = BF16 if br % 16 == 0 else F32
    bk = 2 * kb
    nb = n_keys // bk
    group = 4 if heads % 4 == 0 else 1
    parts = 4 if heads % 4 == 0 else 1
    vmem, dma = pltpu.VMEM, pltpu.SemaphoreType.DMA
    in_vmem, in_hbm = pl.BlockSpec(memory_space=pltpu.VMEM), pl.BlockSpec(memory_space=pl.ANY)
    dq, dk = pl.pallas_call(
        functools.partial(kernel, ns, nh, heads, iheads, idim ** (-0.5), group),
        out_shape=(
            jax.ShapeDtypeStruct((t * iheads, idim), BF16),
            jax.ShapeDtypeStruct((kb, idim), F32),
        ),
        in_specs=[in_hbm, in_vmem, in_vmem, in_hbm, in_vmem, in_vmem,
                  pl.BlockSpec(memory_space=pltpu.SMEM)],
        out_specs=(in_hbm, in_vmem),
        scratch_shapes=[
            vmem((heads, width, t), BF16),
            vmem((t * iheads, idim), BF16),
            vmem((n_keys, width), BF16),
            vmem((n_keys, idim), BF16),
            vmem((nh, cr * iheads, n_keys), F32),
            vmem((t, iheads), F32),
            vmem((bk, t), F32),
            vmem((half, cr, n_keys), F32),
            vmem((half, cr, n_keys), F32),
            vmem((half, cr, n_keys), F32),
            vmem((half, cr, n_keys), F32),
            vmem((nb, t // 2, bk), BF16),
            vmem((nb, t // 2, bk), BF16),
            vmem((nb, t // 2, bk), F32),
            vmem((nb, t // 2, bk), BF16),
            vmem((half, nb, cr, bk), BF16),
            vmem((nh, cr, n_keys), BF16),
            vmem((t * iheads, n_keys), BF16),
            vmem((t * iheads, idim), BF16),
            vmem((idim, n_keys), F32),
            vmem((ns, idim, kb), BF16),
            vmem((ns, idim, kb), BF16),
            vmem((idim, kb), wire),
            vmem((nh, br, kb), wire),
            vmem((idim, kb), wire),
            dma((parts,)), dma, dma((nh,)), dma((ns,)), dma((ns,)), dma((ns,)), dma((ns,)),
            dma((half,)), dma((half,)), dma((nb,)), dma((nb,)),
            dma((half,)), dma((half,)), dma((nb, half)), dma((nb, half)),
            dma((half,)), dma((half,)), dma((nh,)),
            dma((ns,)), dma((ns,)), dma((nh,)), dma((nh,)), dma((nh,)), dma((nh,)),
        ],
        compiler_params=pltpu.CompilerParams(
            collective_id=0, has_side_effects=True, vmem_limit_bytes=60 * 1024 * 1024
        ),
    )(
        query_latent.transpose(1, 2, 0), key_latent.T, normalizer.T,
        index_query.reshape(t * iheads, idim), index_key, index_weight.T, kept,
    )
    dq = dq.reshape(t, iheads, idim)
    return (dq[:, :ihead] if iheads != ihead else dq), dk


def solution(mesh):
    ns, nh = mesh.shape["seq"], mesh.shape["head"]
    return jax.shard_map(
        functools.partial(local, ns, nh),
        mesh=mesh,
        in_specs=(
            P("seq", "head", None),
            P("seq", None),
            P("seq", "head"),
            P("seq", "head", None),
            P("seq", None),
            P("seq", "head"),
            P("seq", None),
        ),
        out_specs=(P("seq", "head", None), P("seq", None)),
        check_vma=False,
    )
```

```python
import functools
import jax
import jax.numpy as jnp
from jax import lax
from jax.experimental import pallas as pl
from jax.experimental.pallas import tpu as pltpu
from jax.sharding import PartitionSpec as P

attn_scale = 192.0 ** (-0.5)
MESH = pl.DeviceIdType.MESH
F32 = jnp.float32
BF16 = jnp.bfloat16


def dot(a, b, ca, cb):
    return lax.dot_general(a, b, (((ca,), (cb,)), ((), ())), preferred_element_type=F32)


def kernel(
    ns, nh, heads, iheads, index_scale, group,
    q_hbm, kl_hbm, nrm_hbm, iq_hbm, ik_hbm, w_hbm, kept_ref,
    dq_hbm, dk_ref,
    nrm_ref, w_ref, klt, qbuf, iq_ref, klat, keys, wm, w_col, hacc,
    s1l, r1l, s2l, r2l, s1h, r1h, own_h, s2h, r2h, gall, dz_ref, dq_ref, acc,
    sa, ra, sb, rb, rc,
    q_sem, iq_sem, in_sem, dq_sem, ik_send, ik_recv, kl_send, kl_fsend, kl_recv,
    l1_send, l1_recv, h1_send, h1_recv, l2_send, l2_recv, h2_send, h2_recv,
    g_send, g_fsend, g_recv, a_send, a_recv, b_send, b_recv, c_send, c_recv,
):
    me_s, me_h = lax.axis_index("seq"), lax.axis_index("head")
    half = nh // 2
    mz, mx = me_h // 2, me_h % 2
    px = 1 - mx
    pair = mz * 2 + px
    n_keys, kb = klat.shape[0], ik_hbm.shape[0]
    cr = r1l.shape[1]
    hr = cr * half
    wr = cr * iheads
    nb, bk = s1h.shape[0], s1h.shape[2]

    def copy(src, dst, ss, rs, s, h):
        return pltpu.make_async_remote_copy(
            src_ref=src, dst_ref=dst, send_sem=ss, recv_sem=rs,
            device_id=(s, h), device_id_type=MESH,
        )

    barrier = pltpu.get_barrier_semaphore()
    for d in range(1, ns):
        pl.semaphore_signal(barrier, inc=1, device_id=((me_s + d) % ns, me_h), device_id_type=MESH)
    for d in range(1, nh):
        pl.semaphore_signal(barrier, inc=1, device_id=(me_s, (me_h + d) % nh), device_id_type=MESH)

    def own_rows(s):
        return pl.ds(pl.multiple_of(s * kb, kb), kb)

    ik_own = pltpu.make_async_copy(ik_hbm, keys.at[own_rows(me_s)], in_sem.at[0])
    w_copy = pltpu.make_async_copy(w_hbm, w_ref, in_sem.at[1])
    kl_own = pltpu.make_async_copy(kl_hbm, klt.at[me_s], in_sem.at[2])
    nrm_copy = pltpu.make_async_copy(nrm_hbm, nrm_ref, in_sem.at[3])
    iq_copy = pltpu.make_async_copy(iq_hbm, iq_ref, iq_sem)
    ik_own.start()
    w_copy.start()
    iq_copy.start()
    kl_own.start()
    nrm_copy.start()
    q_parts = q_sem.shape[0]
    qh = heads // q_parts

    def q_copy(i):
        return pltpu.make_async_copy(
            q_hbm.at[pl.ds(i * qh, qh)], qbuf.at[pl.ds(i * qh, qh)], q_sem.at[i]
        )

    for i in range(q_parts):
        q_copy(i).start()
    pl.semaphore_wait(barrier, ns - 1 + nh - 1)

    chips = ns // 2
    mp, mc = me_s // 2, me_s % 2
    other = mp * 2 + 1 - mc

    def ik_copy(d, s):
        return copy(ik_hbm, keys.at[own_rows(s)], ik_send.at[d], ik_recv.at[s], (me_s + d) % ns, me_h)

    def kl_copy(d, s):
        return copy(kl_hbm, klt.at[s], kl_send.at[d], kl_recv.at[s], ((mp + d) % chips) * 2 + mc, me_h)

    def kl_pair(s):
        return copy(kl_hbm, klt.at[s], kl_send.at[0], kl_recv.at[s], other, me_h)

    def kl_pass(d, s):
        return copy(klt.at[s], klt.at[s], kl_fsend.at[d], kl_recv.at[s], other, me_h)

    for d in range(1, ns):
        ik_copy(d, me_s).start()
    for d in range(1, chips):
        kl_copy(d, me_s).start()
    kl_pair(me_s).start()
    ik_own.wait()
    w_copy.wait()
    w_col[...] = w_ref[...].T
    iq_copy.wait()
    for d in range(1, ns):
        ik_copy(d, (me_s + d) % ns).wait_recv()

    def l1_copy(zt):
        return copy(s1l.at[zt], r1l.at[zt], l1_send.at[zt], l1_recv.at[zt], me_s, pair)

    def l2_copy(zt, frm):
        return copy(s2l.at[zt], r2l.at[frm], l2_send.at[zt], l2_recv.at[frm], me_s, zt * 2 + mx)

    def h1_copy(b):
        return copy(s1h.at[b], r1h.at[b], h1_send.at[b], h1_recv.at[b], me_s, pair)

    def h2_copy(b, zt, frm):
        rows = pl.ds(pl.multiple_of(zt * cr, cr), cr)
        return copy(
            s2h.at[b, rows], r2h.at[frm, b], h2_send.at[b, zt], h2_recv.at[b, frm], me_s, zt * 2 + mx
        )

    def z_step(i, _):
        zt = (mz + 1 + i) % half
        k = jnp.where(i < half, px, mx) * half + zt
        rows = pl.ds(pl.multiple_of(k * cr, cr), cr)
        wide = pl.ds(pl.multiple_of(k * wr, wr), wr)
        z = dot(iq_ref[wide, :], keys[...], 1, 1).reshape(cr, iheads, n_keys)
        wide_w = jnp.broadcast_to(w_col[rows, :][:, None, :], (cr, iheads, iheads))
        sub = lax.broadcasted_iota(jnp.int32, (cr, iheads, iheads), 1)
        lane = lax.broadcasted_iota(jnp.int32, (cr, iheads, iheads), 2)
        w = jnp.sum(jnp.where(sub == lane, wide_w, 0.0), axis=2, keepdims=True)
        part = jnp.where(z > 0, w, 0.0)
        wm[k] = part.reshape(wr, n_keys)
        logit = jnp.sum(part * z, axis=1) * index_scale

        @pl.when(i < half)
        def _():
            s1l[zt] = logit
            l1_copy(zt).start()

        @pl.when(i >= half)
        def _():
            s2l[zt] = logit

        return 0

    lax.fori_loop(0, half, z_step, 0)
    for d in range(1, chips):
        frm = ((mp + d) % chips) * 2 + mc
        kl_copy(d, frm).wait_recv()
        kl_pass(d, frm).start()
    lax.fori_loop(half, nh, z_step, 0)

    kl_own.wait()
    nrm_copy.wait()
    for d in range(chips):
        here = ((mp + d) % chips) * 2 + mc
        klat[own_rows(here), :] = klt[here].T
    for d in range(chips):
        there = ((mp + d) % chips) * 2 + 1 - mc
        kl_pass(d, there).wait_recv()
        klat[own_rows(there), :] = klt[there].T
    for i in range(q_parts):
        q_copy(i).wait()

    def half_rows(x):
        return pl.ds(pl.multiple_of(x * hr, hr), hr)

    def pass_logits():
        for d in range(1, half + 1):
            zt = (mz + d) % half
            l1_copy(zt).wait_recv()
            s2l[zt] = s2l[zt] + r1l[zt]
            if d < half:
                l2_copy(zt, mz).start()

    def pass_sums(b):
        h1_copy(b).wait_recv()
        s2h[b] = (own_h[b] + r1h[b].astype(F32)).astype(BF16)
        for d in range(1, half):
            h2_copy(b, (mz + d) % half, mz).start()

    for b in range(nb):
        hacc[...] = jnp.zeros_like(hacc)

        def score_step(i, _):
            total = hacc[...]
            for j in range(group):
                h = i * group + j
                s = dot(klat[b * bk:(b + 1) * bk, :], qbuf[h], 1, 0)
                total = total + jnp.exp(s * attn_scale - nrm_ref[pl.ds(h, 1), :])
            hacc[...] = total
            return 0

        lax.fori_loop(0, heads // group, score_step, 0)
        turned = hacc[...].T
        low, high = turned[:hr], turned[hr:]
        s1h[b] = jnp.where(px == 0, low, high).astype(BF16)
        h1_copy(b).start()
        own_h[b] = jnp.where(mx == 0, low, high)
        if b == 0:
            pass_logits()
        if b > 0:
            pass_sums(b - 1)
    pass_sums(nb - 1)

    logit = s2l[mz]
    for d in range(1, half):
        frm = (mz + half - d) % half
        l2_copy(frm, frm).wait_recv()
        logit = logit + r2l[frm]

    mine = mx * half + mz
    tile_rows = (cr * nh) // kept_ref.shape[0]
    tile_at = (mine * cr) // tile_rows
    kt = n_keys // kept_ref.shape[1]
    keep = jnp.concatenate(
        [jnp.full((cr, kt), kept_ref[tile_at, j], jnp.int32) for j in range(kept_ref.shape[1])],
        axis=1,
    ) > 0
    top = jnp.max(jnp.where(keep, logit, -jnp.inf), axis=1, keepdims=True)
    expo = jnp.where(keep, jnp.exp(jnp.where(keep, logit, top) - top), 0.0)
    iprob = expo / jnp.sum(expo, axis=1, keepdims=True)

    sums = []
    for b in range(nb):
        value = s2h[b, pl.ds(pl.multiple_of(mz * cr, cr), cr)].astype(F32)
        for d in range(1, half):
            frm = (mz + half - d) % half
            h2_copy(b, frm, frm).wait_recv()
            value = value + r2h[frm, b].astype(F32)
        sums.append(value)
    head_sum = jnp.where(keep, jnp.concatenate(sums, axis=1), 0.0)
    target = head_sum / jnp.sum(head_sum, axis=1, keepdims=True)
    gall[mine] = (iprob - target).astype(BF16)

    def g_copy(d, k):
        zt = (mz + d) % half
        return copy(gall.at[k], gall.at[k], g_send.at[d], g_recv.at[k], me_s, zt * 2 + mx)

    def g_pass(d, k):
        return copy(gall.at[k], gall.at[k], g_fsend.at[d], g_recv.at[k], me_s, pair)

    for d in range(1, half):
        g_copy(d, mine).start()
    g_pass(0, mine).start()

    acc[...] = jnp.zeros_like(acc)

    def back_step(i, _):
        zt = (mz + half - i % half) % half
        k = jnp.where(i < half, mx, px) * half + zt

        @pl.when(jnp.logical_and(i > 0, i < half))
        def _():
            g_copy(i, k).wait_recv()
            g_pass(i, k).start()

        @pl.when(i >= half)
        def _():
            g_pass(i - half, k).wait_recv()

        wide = pl.ds(pl.multiple_of(k * wr, wr), wr)
        g = gall[k].astype(F32)
        dz = (g[:, None, :] * wm[k].reshape(cr, iheads, n_keys)).astype(BF16).reshape(wr, n_keys)
        dz_ref[wide, :] = dz
        acc[...] += dot(iq_ref[wide, :], dz, 0, 0)
        return 0

    lax.fori_loop(0, nh, back_step, 0)

    wire = sb.dtype
    br = rb.shape[1]

    def a_copy(d, s):
        return copy(sa.at[d], ra.at[s], a_send.at[d], a_recv.at[s], (me_s + d) % ns, me_h)

    for d in range(1, ns):
        sa[d] = (acc[:, own_rows((me_s + d) % ns)] * index_scale).astype(BF16)
        a_copy(d, me_s).start()

    def dq_copy(i):
        wide = pl.ds(i * wr, wr)
        return pltpu.make_async_copy(dq_ref.at[wide], dq_hbm.at[wide], dq_sem.at[i])

    def dq_step(i, _):
        wide = pl.ds(pl.multiple_of(i * wr, wr), wr)
        dq_ref[wide, :] = (dot(dz_ref[wide, :], keys[...], 1, 0) * index_scale).astype(BF16)
        dq_copy(i).start()
        return 0

    lax.fori_loop(0, half, dq_step, 0)

    total = acc[:, own_rows(me_s)] * index_scale
    for d in range(1, ns):
        a_copy(d, (me_s + d) % ns).wait_recv()
        total = total + ra[(me_s + d) % ns].astype(F32)
    sb[...] = total.astype(wire)

    def b_rows(h):
        return pl.ds(pl.multiple_of(h * br, br), br)

    def b_copy(d, h):
        to = (me_h + d) % nh
        return copy(sb.at[b_rows(to)], rb.at[h], b_send.at[d], b_recv.at[h], me_s, to)

    def c_copy(d, h):
        return copy(rc.at[b_rows(h)], rc.at[b_rows(h)], c_send.at[d], c_recv.at[h], me_s, (me_h + d) % nh)

    for d in range(1, nh):
        b_copy(d, me_h).start()

    lax.fori_loop(half, nh, dq_step, 0)

    piece = sb[b_rows(me_h), :].astype(F32)
    for d in range(1, nh):
        frm = (me_h + d) % nh
        b_copy(d, frm).wait_recv()
        piece = piece + rb[frm].astype(F32)
    rc[b_rows(me_h), :] = piece.astype(wire)
    for d in range(1, nh):
        c_copy(d, me_h).start()
    for d in range(1, nh):
        c_copy(d, (me_h + d) % nh).wait_recv()
    dk_ref[...] = rc[...].astype(F32).T

    for i in range(nh):
        dq_copy(i).wait()
    for d in range(1, ns):
        ik_copy(d, me_s).wait_send()
        a_copy(d, me_s).wait_send()
    kl_pair(me_s).wait_send()
    for d in range(1, chips):
        kl_copy(d, me_s).wait_send()
        kl_pass(d, me_s).wait_send()
    for i in range(half):
        l1_copy(i).wait_send()
        g_pass(i, mine).wait_send()
    for b in range(nb):
        h1_copy(b).wait_send()
    for d in range(1, half):
        zt = (mz + d) % half
        l2_copy(zt, mz).wait_send()
        g_copy(d, mine).wait_send()
        for b in range(nb):
            h2_copy(b, zt, mz).wait_send()
    for d in range(1, nh):
        b_copy(d, me_h).wait_send()
        c_copy(d, me_h).wait_send()


def hand_over(dq_in, dk_in, dq_out, dk_out, sem):
    first = pltpu.make_async_copy(dq_in, dq_out, sem.at[0])
    second = pltpu.make_async_copy(dk_in, dk_out, sem.at[1])
    first.start()
    second.start()
    first.wait()
    second.wait()


def local(ns, nh, query_latent, key_latent, normalizer, index_query, index_key, index_weight, kept):
    t, heads, width = query_latent.shape
    ihead, idim = index_query.shape[1:]
    iheads = -(-ihead // 8) * 8
    if iheads != ihead:
        index_query = jnp.pad(index_query, ((0, 0), (0, iheads - ihead), (0, 0)))
        index_weight = jnp.pad(index_weight, ((0, 0), (0, iheads - ihead)))
    kb = key_latent.shape[0]
    n_keys = kb * ns
    cr, half, br = t // nh, nh // 2, idim // nh
    wire = BF16 if br % 16 == 0 else F32
    bk = 2 * kb
    nb = n_keys // bk
    group = 4 if heads % 4 == 0 else 1
    parts = 4 if heads % 4 == 0 else 1
    vmem, dma = pltpu.VMEM, pltpu.SemaphoreType.DMA
    in_vmem, in_hbm = pl.BlockSpec(memory_space=pltpu.VMEM), pl.BlockSpec(memory_space=pl.ANY)
    dq, dk = pl.pallas_call(
        functools.partial(kernel, ns, nh, heads, iheads, idim ** (-0.5), group),
        out_shape=(
            jax.ShapeDtypeStruct((t * iheads, idim), BF16),
            jax.ShapeDtypeStruct((kb, idim), F32),
        ),
        in_specs=[in_hbm] * 6 + [pl.BlockSpec(memory_space=pltpu.SMEM)],
        out_specs=(in_hbm, in_vmem),
        scratch_shapes=[
            vmem((heads, t), F32),
            vmem((iheads, t), F32),
            vmem((ns, width, kb), BF16),
            vmem((heads, width, t), BF16),
            vmem((t * iheads, idim), BF16),
            vmem((n_keys, width), BF16),
            vmem((n_keys, idim), BF16),
            vmem((nh, cr * iheads, n_keys), F32),
            vmem((t, iheads), F32),
            vmem((bk, t), F32),
            vmem((half, cr, n_keys), F32),
            vmem((half, cr, n_keys), F32),
            vmem((half, cr, n_keys), F32),
            vmem((half, cr, n_keys), F32),
            vmem((nb, t // 2, bk), BF16),
            vmem((nb, t // 2, bk), BF16),
            vmem((nb, t // 2, bk), F32),
            vmem((nb, t // 2, bk), BF16),
            vmem((half, nb, cr, bk), BF16),
            vmem((nh, cr, n_keys), BF16),
            vmem((t * iheads, n_keys), BF16),
            vmem((t * iheads, idim), BF16),
            vmem((idim, n_keys), F32),
            vmem((ns, idim, kb), BF16),
            vmem((ns, idim, kb), BF16),
            vmem((idim, kb), wire),
            vmem((nh, br, kb), wire),
            vmem((idim, kb), wire),
            dma((parts,)), dma, dma((4,)), dma((nh,)), dma((ns,)), dma((ns,)),
            dma((ns // 2,)), dma((ns // 2,)), dma((ns,)),
            dma((half,)), dma((half,)), dma((nb,)), dma((nb,)),
            dma((half,)), dma((half,)), dma((nb, half)), dma((nb, half)),
            dma((half,)), dma((half,)), dma((nh,)),
            dma((ns,)), dma((ns,)), dma((nh,)), dma((nh,)), dma((nh,)), dma((nh,)),
        ],
        compiler_params=pltpu.CompilerParams(
            collective_id=0, has_side_effects=True, vmem_limit_bytes=60 * 1024 * 1024
        ),
    )(
        query_latent.transpose(1, 2, 0), key_latent.T, normalizer.T,
        index_query.reshape(t * iheads, idim), index_key, index_weight.T, kept,
    )
    dq, dk = pl.pallas_call(
        hand_over,
        out_shape=(
            jax.ShapeDtypeStruct((t * iheads, idim), BF16),
            jax.ShapeDtypeStruct((kb, idim), F32),
        ),
        in_specs=[in_hbm] * 2,
        out_specs=(in_hbm, in_hbm),
        scratch_shapes=[dma((2,))],
    )(dq, dk)
    dq = dq.reshape(t, iheads, idim)
    return (dq[:, :ihead] if iheads != ihead else dq), dk


def solution(mesh):
    ns, nh = mesh.shape["seq"], mesh.shape["head"]
    return jax.shard_map(
        functools.partial(local, ns, nh),
        mesh=mesh,
        in_specs=(
            P("seq", "head", None),
            P("seq", None),
            P("seq", "head"),
            P("seq", "head", None),
            P("seq", None),
            P("seq", "head"),
            P("seq", None),
        ),
        out_specs=(P("seq", "head", None), P("seq", None)),
        check_vma=False,
    )
```
